32 devices in a mesh: groups: 2 (over y), section: 4 (over x, core), space: 4 (over z).
Axes of the slice: x: 2, y: 2, z: 4, core: 2. Of those that a mesh axis runs over, the one named last changes fastest.
Arguments:
- layer_inputs: bfloat16 [4, 8192, 512], P('section', ('groups', 'space')), parts along dimension 1, may hold values from -54 to 54
- saved_queries: bfloat16 [4, 128, 64, 512], P('section', ('groups', 'space')), parts along dimension 1, may hold values from -8 to 8
- saved_keys: bfloat16 [4, 128, 64, 512], P('section', ('groups', 'space')), parts along dimension 1, may hold values from -8 to 8
- value_weight: bfloat16 [4, 512, 512], P('section'), may hold values from -0.25 to 0.25
- out_weight: bfloat16 [4, 512, 512], P('section'), may hold values from -0.25 to 0.25
- norm_gain: bfloat16 [4, 512], P('section'), may hold values from 0.099609375 to 1.8984375
- cotangent: bfloat16 [8192, 512], P(('groups', 'space'), 'section'), parts along dimension 0, may hold values from -24 to 24
Outputs:
- input_grad: bfloat16 [8192, 512], P(('groups', 'space'), 'section'), parts along dimension 0
- value_grad: float32 [4, 1024, 512], P('section', ('groups', 'space')), parts along dimension 1
- out_grad: float32 [4, 1024, 512], P('section', ('groups', 'space')), parts along dimension 1
- gain_grad: float32 [4, 1024], P('section', 'groups'), parts along dimension 1
The draws below stay inside these ranges and needn't reach their ends.
There are 2 independent parts, one for each index of `groups`. The reference program is written for one: setup_inputs(seed, part) draws one part's arguments, and reference() takes and returns one part's arrays. A program takes and returns all parts, laid end to end along the dimension named above; an argument that names none is the same for every part. Nothing has to cross between parts.
All inputs are finite; a program needn't handle non-finite values.
Results may differ from the reference program's by a relative error of at most 0.013.
Values may be sent and summed in bfloat16 or wider, within the bound.
A program may use at most 128 MiB of HBM per device.

```python
import jax
import jax.numpy as jnp
from jax import lax

D = 512
HD = 32
COLS = 64
HC = 512
BAND = 16
TOKENS = 4096
NW = 64
SECTIONS = 4
N_SPACE = 4


def draw_pairs(key):
    base = jax.random.fold_in(key, 11)
    first, second = jax.random.split(base, 2)
    shape = (SECTIONS, NW, 64, HC)
    queries = jnp.clip(jax.random.normal(first, shape, jnp.float32), -6.0, 6.0)
    keys_out = jnp.clip(jax.random.normal(second, shape, jnp.float32), -6.0, 6.0)
    return (queries, keys_out)


def draw_saved_queries(key, part):
    return draw_pairs(key)[0].astype(jnp.bfloat16)


def draw_saved_keys(key, part):
    return draw_pairs(key)[1].astype(jnp.bfloat16)


def draw_layer_inputs(key, part):
    first, second, third = jax.random.split(jax.random.fold_in(key, 23), 3)
    shape = (SECTIONS, TOKENS, D)
    drawn = jnp.clip(jax.random.normal(first, shape, jnp.float32), -6.0, 6.0)
    lower, upper = (0.3, 3.0)
    row_scale = jnp.exp(jax.random.uniform(second, (SECTIONS, TOKENS, 1), jnp.float32, jnp.log(lower), jnp.log(upper)))
    col_scale = jnp.exp(jax.random.uniform(third, (SECTIONS, 1, D), jnp.float32, jnp.log(lower), jnp.log(upper)))
    return (drawn * row_scale * col_scale).astype(jnp.bfloat16)


def draw_cotangent(key, part):
    first = jax.random.fold_in(jax.random.fold_in(key, 37), 0)
    height = TOKENS // COLS
    fraction = (jnp.arange(TOKENS) // COLS).astype(jnp.float32) / float(height - 1)
    drawn = jnp.clip(jax.random.normal(first, (TOKENS, D), jnp.float32), -6.0, 6.0)
    rising = jnp.exp(fraction * jnp.log(3.0))
    return (drawn * rising[:, None]).astype(jnp.bfloat16)


def steps_of(own_key, dims, cuts, smallest, top_value):
    gain = 1.0
    for axis_at, parts in cuts:
        heights = jax.random.uniform(jax.random.fold_in(jax.random.fold_in(own_key, 6), axis_at), (parts,), jnp.float32, smallest / len(cuts), top_value / len(cuts))
        gain = gain * jnp.repeat(jnp.exp(heights), dims[axis_at] // parts).reshape((-1,) + (1,) * (len(dims) - 1 - axis_at))
    return gain


def bell_draw(stream_key, shape, spread, most, pieces=(), held_as=jnp.bfloat16):
    entries = jax.random.normal(stream_key, shape, jnp.float32) * spread
    if len(pieces) > 0:
        entries = steps_of(stream_key, shape, pieces, -0.22, 0.18) * entries
    return jnp.clip(entries, min=-most, max=most).astype(held_as)


def setup_inputs(seed: int = 0, part: int = 0) -> dict:
    keys = jax.random.split(jax.random.key(seed), 8)
    part_keys = jax.random.split(jax.random.fold_in(keys[7], part), 8)
    return {
        "layer_inputs": draw_layer_inputs(jax.random.fold_in(jax.random.fold_in(keys[7], part), 71), part),
        "saved_queries": draw_saved_queries(jax.random.fold_in(jax.random.fold_in(keys[7], part), 71), part),
        "saved_keys": draw_saved_keys(jax.random.fold_in(jax.random.fold_in(keys[7], part), 71), part),
        "value_weight": bell_draw(keys[3], (SECTIONS, D, HC), D ** -0.5, 0.25, ((0, 4),)),
        "out_weight": bell_draw(keys[4], (SECTIONS, D, HC), D ** -0.5, 0.25, ((0, 4),)),
        "norm_gain": jnp.clip(1.0 + 0.18 * jax.random.normal(keys[5], (SECTIONS, D), jnp.float32), 0.099609375, 1.8984375).astype(jnp.bfloat16),
        "cotangent": draw_cotangent(jax.random.fold_in(jax.random.fold_in(keys[7], part), 71), part),
    }


epsilon = 1e-06

def to_windows(full):
    width = full.shape[-1]
    depth = BAND // 8 * N_SPACE // 8
    grid = full.reshape(N_SPACE, BAND // 8, 8, 8, COLS // 8, width)
    grid = grid.transpose(2, 4, 0, 1, 3, 5)
    grid = grid.reshape(N_SPACE, COLS // N_SPACE, 8, depth, 8, width)
    grid = grid.transpose(0, 3, 1, 2, 4, 5)
    return grid.reshape(NW, 64, width)

def from_windows(grid):
    width = grid.shape[-1]
    depth = BAND // 8 * N_SPACE // 8
    full = grid.reshape(N_SPACE, depth, COLS // N_SPACE, 8, 8, width)
    full = full.transpose(0, 2, 3, 1, 4, 5)
    full = full.reshape(8, COLS // 8, N_SPACE, BAND // 8, 8, width)
    full = full.transpose(2, 3, 0, 4, 1, 5)
    return full.reshape(TOKENS, width)

def window_probs(queries, keys_in):
    heads = HC // HD
    qv = queries.astype(jnp.float32).reshape(NW, 64, heads, HD)
    kv = keys_in.astype(jnp.float32).reshape(NW, 64, heads, HD)
    scores = jnp.einsum('wqhd,wkhd->whqk', qv, kv) * HD ** (-0.5)
    return jax.nn.softmax(scores, axis=-1).astype(jnp.bfloat16)

def attend(probs, grid):
    heads = HC // HD
    vw = grid.astype(jnp.float32).reshape(NW, 64, heads, HD)
    out = jnp.einsum('whqk,wkhd->wqhd', probs.astype(jnp.float32), vw)
    return out.reshape(NW, 64, HC).astype(jnp.bfloat16)

def attend_back(probs, grid):
    heads = HC // HD
    gw = grid.astype(jnp.float32).reshape(NW, 64, heads, HD)
    out = jnp.einsum('whqk,wqhd->wkhd', probs.astype(jnp.float32), gw)
    return out.reshape(NW, 64, HC).astype(jnp.bfloat16)

def reference(layer_inputs, saved_queries, saved_keys, value_weight, out_weight, norm_gain, cotangent):
    factor = float(TOKENS) ** (-0.5)
    stored = []
    for layer in range(SECTIONS):
        xf = layer_inputs[layer].astype(jnp.float32)
        rstd = 1.0 / jnp.sqrt(lax.optimization_barrier(jnp.mean(xf * xf, axis=-1, keepdims=True)) + epsilon)
        normed = xf * rstd
        gains = norm_gain[layer].astype(jnp.float32)
        hidden = (normed * gains).astype(jnp.bfloat16)
        values = jnp.dot(hidden, value_weight[layer], preferred_element_type=jnp.float32).astype(jnp.bfloat16)
        probs = window_probs(saved_queries[layer], saved_keys[layer])
        attended = from_windows(attend(probs, to_windows(values)))
        stored.append((rstd, normed, gains, hidden, probs, attended))
    value_grads = [None] * SECTIONS
    out_grads = [None] * SECTIONS
    gain_grads = [None] * SECTIONS
    cot = cotangent
    for layer in reversed(range(SECTIONS)):
        rstd, normed, gains, hidden, probs, attended = stored[layer]
        grad_attn = jnp.dot(cot, out_weight[layer], preferred_element_type=jnp.float32).astype(jnp.bfloat16)
        grad_values = from_windows(attend_back(probs, to_windows(grad_attn)))
        grad_norm = jnp.dot(grad_values, value_weight[layer].T, preferred_element_type=jnp.float32)
        dxn = grad_norm * gains
        total = cot.astype(jnp.float32) + rstd * (dxn - normed * lax.optimization_barrier(jnp.mean(dxn * normed, axis=-1, keepdims=True)))
        value_grads[layer] = jnp.dot(hidden.T, grad_values, preferred_element_type=jnp.float32) * factor
        out_grads[layer] = jnp.dot(cot.T, attended, preferred_element_type=jnp.float32) * factor
        gain_grads[layer] = lax.optimization_barrier(jnp.sum(grad_norm * normed, axis=0)) * factor
        cot = total.astype(jnp.bfloat16)
    return (cot, jnp.stack(value_grads), jnp.stack(out_grads), jnp.stack(gain_grads))
```

```python
import jax
import jax.numpy as jnp
from jax import lax
from jax.sharding import PartitionSpec as P

HD = 32
COLS = 64


epsilon = 1e-06


def shifted(block, axis, distance):
    devices = range(lax.axis_size(axis))
    route = [(i - distance, i) for i in devices if i - distance in devices]
    return lax.ppermute(block, axis, route)


def to_pieces(rows_in, band, spaces):
    width = rows_in.shape[-1]
    blocks = rows_in.reshape(band // 8, 8, 8, COLS // 8, width).transpose(1, 3, 0, 2, 4)
    return blocks.reshape(spaces, COLS // spaces, band // 8, 8, width)


def from_pieces(pieces, band, spaces):
    width = pieces.shape[-1]
    depth = band // 8 * spaces // 8
    blocks = pieces.transpose(0, 2, 1, 3, 4).reshape(8, depth, COLS // spaces, 8, width)
    return blocks.transpose(1, 2, 0, 3, 4).reshape(-1, width)


def to_window_pieces(rows_in, band, spaces):
    width = rows_in.shape[-1]
    depth = band // 8 * spaces // 8
    blocks = rows_in.reshape(depth, COLS // spaces, 8, 8, width).transpose(2, 0, 1, 3, 4)
    return blocks.reshape(spaces, band // 8, COLS // spaces, 8, width).transpose(0, 2, 1, 3, 4)


def from_window_pieces(pieces, band):
    width = pieces.shape[-1]
    blocks = pieces.reshape(8, COLS // 8, band // 8, 8, width).transpose(2, 0, 3, 1, 4)
    return blocks.reshape(-1, width)


def window_probs(queries, keys_in):
    count = queries.shape[0]
    heads = queries.shape[-1] // HD
    qv = queries.reshape(count, 64, heads, HD)
    kv = keys_in.reshape(count, 64, heads, HD)
    scores = jnp.einsum("wqhd,wkhd->whqk", qv, kv, preferred_element_type=jnp.float32) * HD ** (
        -0.5
    )
    return jax.nn.softmax(scores, axis=-1).astype(jnp.bfloat16)


def attend(probs, values):
    count = probs.shape[0]
    heads = probs.shape[1]
    grid = values.reshape(count, 64, heads, -1)
    out = jnp.einsum("whqk,wkhd->wqhd", probs, grid, preferred_element_type=jnp.float32)
    return out.reshape(count * 64, -1).astype(jnp.bfloat16)


def attend_back(probs, grads):
    count = probs.shape[0]
    heads = probs.shape[1]
    grid = grads.reshape(count, 64, heads, -1)
    out = jnp.einsum("whqk,wqhd->wkhd", probs, grid, preferred_element_type=jnp.float32)
    return out.reshape(count * 64, -1).astype(jnp.bfloat16)


def inverse_rms(values):
    floats = values.astype(jnp.float32)
    return 1.0 / jnp.sqrt(jnp.mean(floats * floats, axis=-1, keepdims=True) + epsilon)


def local(layer_inputs, saved_queries, saved_keys, value_weight, out_weight, norm_gain, cotangent):
    sections = lax.axis_size("section")
    spaces = lax.axis_size("space")
    section_index = lax.axis_index("section")
    inputs = layer_inputs[0]
    w_value = value_weight[0]
    w_out = out_weight[0]
    gains = norm_gain[0].astype(jnp.float32)
    tok_rows = inputs.shape[0]
    width = inputs.shape[1]
    band = tok_rows // COLS
    factor = float(tok_rows * spaces) ** (-0.5)
    probs = window_probs(saved_queries[0], saved_keys[0])

    def exchange(block):
        return lax.all_to_all(block, "space", split_axis=0, concat_axis=0, tiled=True)

    def to_windows(rows_in):
        return from_pieces(exchange(to_pieces(rows_in, band, spaces)), band, spaces)

    def to_bands(rows_in):
        return from_window_pieces(exchange(to_window_pieces(rows_in, band, spaces)), band)

    cot = lax.all_gather(to_windows(cotangent), "section", axis=1, tiled=True)
    inputs = to_windows(inputs)
    rstd = inverse_rms(inputs)
    normed = inputs.astype(jnp.float32) * rstd
    hidden = (normed * gains).astype(jnp.bfloat16)
    values = jnp.dot(hidden, w_value, preferred_element_type=jnp.float32).astype(jnp.bfloat16)
    attended = attend(probs, values)
    keep_values = jnp.zeros((tok_rows, w_value.shape[1]), jnp.bfloat16)
    keep_cot = jnp.zeros((tok_rows, width), jnp.bfloat16)
    result = cot
    for layer_step in range(sections):
        grad_attn = jnp.dot(cot, w_out, preferred_element_type=jnp.float32).astype(jnp.bfloat16)
        grad_values = attend_back(probs, grad_attn)
        grad_norm = lax.dot_general(
            grad_values, w_value, (((1,), (1,)), ((), ())), preferred_element_type=jnp.float32
        )
        scaled = grad_norm * gains
        total = cot.astype(jnp.float32) + rstd * (
            scaled - normed * jnp.mean(scaled * normed, axis=-1, keepdims=True)
        )
        active = section_index == sections - 1 - layer_step
        keep_values = jnp.where(active, grad_values, keep_values)
        keep_cot = jnp.where(active, cot, keep_cot)
        result = total.astype(jnp.bfloat16)
        if layer_step + 1 < sections:
            cot = shifted(result, "section", -1)
    quarter = width // sections
    split = result.reshape(tok_rows, sections, quarter).transpose(1, 0, 2)
    mine = lax.all_to_all(split, "section", split_axis=0, concat_axis=0, tiled=True)[0]
    input_grad = to_bands(mine)
    kept_norm = lax.dot_general(
        keep_values, w_value, (((1,), (1,)), ((), ())), preferred_element_type=jnp.float32
    )
    gain_part = jnp.sum(kept_norm * normed, axis=0)
    first = lax.dot_general(
        hidden, keep_values, (((0,), (0,)), ((), ())), preferred_element_type=jnp.float32
    )
    second = lax.dot_general(
        keep_cot, attended, (((0,), (0,)), ((), ())), preferred_element_type=jnp.float32
    )
    totals = lax.psum_scatter(
        jnp.concatenate([first, second], axis=1) * factor, "space", scatter_dimension=0, tiled=True
    )
    channels = w_value.shape[1]
    value_grad = totals[:, :channels][None]
    out_grad = totals[:, channels:][None]
    gain_grad = lax.psum(gain_part * factor, "space")[None]
    return (input_grad, value_grad, out_grad, gain_grad)


def solution(mesh):
    in_specs = (
        P("section", ("groups", "space"), None),
        P("section", ("groups", "space"), None, None),
        P("section", ("groups", "space"), None, None),
        P("section", None, None),
        P("section", None, None),
        P("section", None),
        P(("groups", "space"), "section"),
    )
    out_specs = (
        P(("groups", "space"), "section"),
        P("section", ("groups", "space"), None),
        P("section", ("groups", "space"), None),
        P("section", "groups"),
    )
    return jax.shard_map(local, mesh=mesh, in_specs=in_specs, out_specs=out_specs, check_vma=False)
```

```python
import functools

import jax
import jax.numpy as jnp
from jax import lax
from jax.experimental import pallas as pl
from jax.experimental.pallas import tpu as pltpu
from jax.sharding import PartitionSpec as P

HD = 32
COLS = 64


epsilon = 1e-06


def shifted(block, axis, distance):
    devices = range(lax.axis_size(axis))
    route = [(i - distance, i) for i in devices if i - distance in devices]
    return lax.ppermute(block, axis, route)


def to_pieces(rows_in, band, spaces):
    width = rows_in.shape[-1]
    blocks = rows_in.reshape(band // 8, 8, 8, COLS // 8, width).transpose(1, 3, 0, 2, 4)
    return blocks.reshape(spaces, COLS // spaces, band // 8, 8, width)


def from_pieces(pieces, band, spaces):
    width = pieces.shape[-1]
    depth = band // 8 * spaces // 8
    blocks = pieces.transpose(0, 2, 1, 3, 4).reshape(8, depth, COLS // spaces, 8, width)
    return blocks.transpose(1, 2, 0, 3, 4).reshape(-1, width)


def to_window_pieces(rows_in, band, spaces):
    width = rows_in.shape[-1]
    depth = band // 8 * spaces // 8
    blocks = rows_in.reshape(depth, COLS // spaces, 8, 8, width).transpose(2, 0, 1, 3, 4)
    return blocks.reshape(spaces, band // 8, COLS // spaces, 8, width).transpose(0, 2, 1, 3, 4)


def from_window_pieces(pieces, band):
    width = pieces.shape[-1]
    blocks = pieces.reshape(8, COLS // 8, band // 8, 8, width).transpose(2, 0, 3, 1, 4)
    return blocks.reshape(-1, width)


def window_probs(queries, keys_in):
    count = queries.shape[0]
    heads = queries.shape[-1] // HD
    qv = queries.reshape(count, 64, heads, HD)
    kv = keys_in.reshape(count, 64, heads, HD)
    scores = jnp.einsum("wqhd,wkhd->whqk", qv, kv, preferred_element_type=jnp.float32) * HD ** (
        -0.5
    )
    return jax.nn.softmax(scores, axis=-1).astype(jnp.bfloat16)


def attend(probs, values):
    count = probs.shape[0]
    heads = probs.shape[1]
    grid = values.reshape(count, 64, heads, -1)
    out = jnp.einsum("whqk,wkhd->wqhd", probs, grid, preferred_element_type=jnp.float32)
    return out.reshape(count * 64, -1).astype(jnp.bfloat16)


def attend_back(probs, grads):
    count = probs.shape[0]
    heads = probs.shape[1]
    grid = grads.reshape(count, 64, heads, -1)
    out = jnp.einsum("whqk,wqhd->wkhd", probs, grid, preferred_element_type=jnp.float32)
    return out.reshape(count * 64, -1).astype(jnp.bfloat16)


def inverse_rms(values):
    floats = values.astype(jnp.float32)
    return 1.0 / jnp.sqrt(jnp.mean(floats * floats, axis=-1, keepdims=True) + epsilon)


def local_plain(layer_inputs, saved_queries, saved_keys, value_weight, out_weight, norm_gain, cotangent):
    sections = lax.axis_size("section")
    spaces = lax.axis_size("space")
    section_index = lax.axis_index("section")
    inputs = layer_inputs[0]
    w_value = value_weight[0]
    w_out = out_weight[0]
    gains = norm_gain[0].astype(jnp.float32)
    tok_rows = inputs.shape[0]
    width = inputs.shape[1]
    band = tok_rows // COLS
    factor = float(tok_rows * spaces) ** (-0.5)
    probs = window_probs(saved_queries[0], saved_keys[0])

    def exchange(block):
        return lax.all_to_all(block, "space", split_axis=0, concat_axis=0, tiled=True)

    def to_windows(rows_in):
        return from_pieces(exchange(to_pieces(rows_in, band, spaces)), band, spaces)

    def to_bands(rows_in):
        return from_window_pieces(exchange(to_window_pieces(rows_in, band, spaces)), band)

    cot = lax.all_gather(to_windows(cotangent), "section", axis=1, tiled=True)
    inputs = to_windows(inputs)
    rstd = inverse_rms(inputs)
    normed = inputs.astype(jnp.float32) * rstd
    hidden = (normed * gains).astype(jnp.bfloat16)
    values = jnp.dot(hidden, w_value, preferred_element_type=jnp.float32).astype(jnp.bfloat16)
    attended = attend(probs, values)
    keep_values = jnp.zeros((tok_rows, w_value.shape[1]), jnp.bfloat16)
    keep_cot = jnp.zeros((tok_rows, width), jnp.bfloat16)
    result = cot
    for layer_step in range(sections):
        grad_attn = jnp.dot(cot, w_out, preferred_element_type=jnp.float32).astype(jnp.bfloat16)
        grad_values = attend_back(probs, grad_attn)
        grad_norm = lax.dot_general(
            grad_values, w_value, (((1,), (1,)), ((), ())), preferred_element_type=jnp.float32
        )
        scaled = grad_norm * gains
        total = cot.astype(jnp.float32) + rstd * (
            scaled - normed * jnp.mean(scaled * normed, axis=-1, keepdims=True)
        )
        active = section_index == sections - 1 - layer_step
        keep_values = jnp.where(active, grad_values, keep_values)
        keep_cot = jnp.where(active, cot, keep_cot)
        result = total.astype(jnp.bfloat16)
        if layer_step + 1 < sections:
            cot = shifted(result, "section", -1)
    quarter = width // sections
    split = result.reshape(tok_rows, sections, quarter).transpose(1, 0, 2)
    mine = lax.all_to_all(split, "section", split_axis=0, concat_axis=0, tiled=True)[0]
    input_grad = to_bands(mine)
    kept_norm = lax.dot_general(
        keep_values, w_value, (((1,), (1,)), ((), ())), preferred_element_type=jnp.float32
    )
    gain_part = jnp.sum(kept_norm * normed, axis=0)
    first = lax.dot_general(
        hidden, keep_values, (((0,), (0,)), ((), ())), preferred_element_type=jnp.float32
    )
    second = lax.dot_general(
        keep_cot, attended, (((0,), (0,)), ((), ())), preferred_element_type=jnp.float32
    )
    totals = lax.psum_scatter(
        jnp.concatenate([first, second], axis=1) * factor, "space", scatter_dimension=0, tiled=True
    )
    channels = w_value.shape[1]
    value_grad = totals[:, :channels][None]
    out_grad = totals[:, channels:][None]
    gain_grad = lax.psum(gain_part * factor, "space")[None]
    return (input_grad, value_grad, out_grad, gain_grad)


MESH = pl.DeviceIdType.MESH
CHUNKS = 4
F32 = jnp.float32
BF16 = jnp.bfloat16


def dot(left, right, contract):
    return lax.dot_general(left, right, ((contract[:1], contract[1:]), ((), ())),
                           preferred_element_type=F32)


def fused(sections, spaces, reps, factor,
          x_ref, q_ref, k_ref, wv_ref, wo_ref, gain_ref, cot_ref,
          ig_ref, vg_ref, og_ref, gg_ref,
          xs, xr, cs, cr, ch, res, pt, vacc, oacc, gacc, iso, iri, ws, wr, gr,
          x_ss, x_rs, c_ss, c_rs, h_ss, h_rs, i_ss, i_rs, w_ss, w_rs, g_ss, g_rs):
    sec = lax.axis_index("section")
    z = lax.axis_index("space")
    last = sections - 1
    tile = reps * 8
    windows = q_ref.shape[0]
    wc = windows // CHUNKS
    rows = wc * 64
    crow = wc * tile
    width = x_ref.shape[1]
    quarter = cot_ref.shape[1]
    groups = width // 128

    def dev(s, zz):
        return {"section": s, "space": zz}

    def around(pos, step, size):
        return lax.rem(pos + step, size)

    def remote(src, dst, ssem, rsem, target):
        return pltpu.make_async_remote_copy(
            src_ref=src, dst_ref=dst, send_sem=ssem, recv_sem=rsem,
            device_id=target, device_id_type=MESH)

    barrier = pltpu.get_barrier_semaphore()
    for a in range(sections):
        for b in range(spaces):
            if a or b:
                pl.semaphore_signal(
                    barrier, inc=1,
                    device_id=dev(around(sec, a, sections), around(z, b, spaces)),
                    device_id_type=MESH)

    size = reps * 64
    shift = tile.bit_length() - 1
    row_at = lax.broadcasted_iota(jnp.int32, (size, size), 0)
    col_at = lax.broadcasted_iota(jnp.int32, (size, size), 1)
    wanted = (((row_at >> 3) & (reps - 1)) << 6) + ((row_at & 7) << 3) + (row_at >> shift)
    perm = jnp.where(wanted == col_at, 1.0, 0.0).astype(BF16)
    blocks = size // crow

    def reorder(y0, ref):
        parts = [ref[pl.ds(pl.multiple_of(r * 512 + y0 * 64, 64), 64), :] for r in range(reps)]
        return dot(perm, jnp.concatenate(parts, axis=0), (1, 0)).astype(BF16)

    def split_cot(y0, carry):
        cs[pl.ds(y0 * blocks, blocks)] = reorder(y0, cot_ref).reshape(blocks, crow, quarter)
        return carry

    def split_x(y0, carry):
        xs[pl.ds(y0 * blocks, blocks)] = reorder(y0, x_ref).reshape(blocks, crow, width)
        return carry

    lax.fori_loop(0, 8, split_cot, 0)
    pl.semaphore_wait(barrier, sections * spaces - 1)

    def cot_copy(b):
        d = around(z, b, spaces)
        return remote(cs.at[pl.ds(d * CHUNKS, CHUNKS)], cr.at[sec, z], c_ss.at[b],
                      c_rs.at[sec * spaces + z], dev(last, d))

    for b in range(1, spaces):
        cot_copy(b).start()

    @pl.when(sec != last)
    def _():
        cot_copy(0).start()

    @pl.when(sec == last)
    def _():
        cr[last, z] = cs[pl.ds(z * CHUNKS, CHUNKS)]

    lax.fori_loop(0, 8, split_x, 0)

    def x_copy(p, c):
        d = around(z, p, spaces)
        return remote(xs.at[d * CHUNKS + c], xr.at[z * CHUNKS + c], x_ss.at[p * CHUNKS + c],
                      x_rs.at[z * CHUNKS + c], dev(sec, d))

    def start_x(c, carry):
        for p in range(1, spaces):
            x_copy(p, c).start()
        return carry

    lax.fori_loop(0, CHUNKS, start_x, 0)
    xr[pl.ds(z * CHUNKS, CHUNKS)] = xs[pl.ds(z * CHUNKS, CHUNKS)]

    lane = lax.broadcasted_iota(jnp.int32, (1, 128), 1)
    per = 128 // HD
    heads = [(lane >= h * HD) & (lane < h * HD + HD) for h in range(per)]
    masks = [jnp.where(m, 1.0, 0.0).astype(BF16) for m in heads]

    def spread(block):
        return jnp.concatenate([block * m for m in masks], axis=0)

    def make_probs(w, carry):
        for g in range(groups):
            at = slice(g * 128, g * 128 + 128)
            scores = dot(k_ref[w, :, at], spread(q_ref[w, :, at]), (1, 1)) * HD ** (-0.5)
            top = jnp.max(scores, axis=0, keepdims=True)
            powers = jnp.exp(scores - top)
            pt[w * groups + g] = (
                powers * (1.0 / jnp.sum(powers, axis=0, keepdims=True))).astype(BF16)
        return carry

    lax.fori_loop(0, windows, make_probs, 0)
    vacc[...] = jnp.zeros_like(vacc)
    oacc[...] = jnp.zeros_like(oacc)
    gacc[...] = jnp.zeros_like(gacc)

    def out_copy(c, a, b):
        d = around(z, b, spaces)
        return remote(iso.at[(c * sections + a) * spaces + d], iri.at[z * CHUNKS + c],
                      i_ss.at[(c * sections + a) * spaces + b], i_rs.at[z * CHUNKS + c],
                      dev(a, d))

    def chain_copy(c):
        return remote(res.at[c], ch.at[c], h_ss.at[c], h_rs.at[c],
                      dev(lax.rem(sec + last, sections), z))

    @pl.when(sec == last)
    def _():
        for a in range(sections):
            for b in range(spaces):
                src = around(z, b, spaces)

                def arrive(a=a, src=src):
                    remote(cs.at[pl.ds(0, CHUNKS)], cr.at[a, src], c_ss.at[0],
                           c_rs.at[a * spaces + src], dev(a, src)).wait_recv()

                if a != last or b != 0:
                    arrive()
        for c in range(CHUNKS):
            for a in range(sections):
                for u in range(wc):
                    ch[c, u * 64:u * 64 + 64, a * quarter:(a + 1) * quarter] = jnp.concatenate(
                        [cr[a, s, c, u * tile:(u + 1) * tile, :] for s in range(spaces)], axis=0)

    def step(c, carry):
        for p in range(1, spaces):
            src = around(z, p, spaces)
            remote(xs.at[0], xr.at[src * CHUNKS + c], x_ss.at[0], x_rs.at[src * CHUNKS + c],
                   dev(sec, src)).wait_recv()
        parts = [xr[s * CHUNKS + c, u * tile:(u + 1) * tile, :]
                 for u in range(wc) for s in range(spaces)]
        xf = jnp.concatenate(parts, axis=0).astype(F32)
        rstd = 1.0 / jnp.sqrt(jnp.mean(xf * xf, axis=-1, keepdims=True) + epsilon)
        normed = xf * rstd
        gains = gain_ref[...].astype(F32)
        hidden = (normed * gains).astype(BF16)
        values = dot(hidden, wv_ref[...], (1, 0)).astype(BF16)
        out_rows = []
        for w in range(wc):
            out_cols = []
            for g in range(groups):
                full = dot(pt[(c * wc + w) * groups + g],
                           values[w * 64:w * 64 + 64, g * 128:g * 128 + 128], (0, 0))
                one = jnp.where(heads[0], full[:64], 0.0)
                for h in range(1, per):
                    one = jnp.where(heads[h], full[h * 64:h * 64 + 64], one)
                out_cols.append(one.astype(BF16))
            out_rows.append(jnp.concatenate(out_cols, axis=1))
        attended = jnp.concatenate(out_rows, axis=0)

        @pl.when(sec != last)
        def _():
            chain_copy(c).wait_recv()

        cot = ch[c]
        grad_attn = dot(cot, wo_ref[...], (1, 0)).astype(BF16)
        out_rows = []
        for w in range(wc):
            out_cols = []
            for g in range(groups):
                out_cols.append(dot(
                    pt[(c * wc + w) * groups + g],
                    spread(grad_attn[w * 64:w * 64 + 64, g * 128:g * 128 + 128]),
                    (1, 0)).astype(BF16))
            out_rows.append(jnp.concatenate(out_cols, axis=1))
        grad_values = jnp.concatenate(out_rows, axis=0)
        grad_norm = dot(grad_values, wv_ref[...], (1, 1))
        product = grad_norm * normed
        mean = jnp.mean(product * gains, axis=-1, keepdims=True)
        total = cot.astype(F32) + rstd * (grad_norm * gains - normed * mean)
        res[c] = total.astype(BF16)

        @pl.when(sec != 0)
        def _():
            chain_copy(c).start()

        @pl.when(sec == 0)
        def _():
            for a in range(sections):
                for s in range(spaces):
                    iso[(c * sections + a) * spaces + s] = jnp.concatenate(
                        [res[c, u * 64 + s * tile:u * 64 + (s + 1) * tile,
                             a * quarter:(a + 1) * quarter] for u in range(wc)], axis=0)
            for a in range(sections):
                for b in range(spaces):
                    if a or b:
                        out_copy(c, a, b).start()
            iri[z * CHUNKS + c] = iso[c * sections * spaces + z]

        gacc[...] += jnp.sum(product, axis=0, keepdims=True)
        oacc[...] += dot(cot, attended, (0, 0))
        vacc[...] += dot(hidden, grad_values, (0, 0))
        return carry

    lax.fori_loop(0, CHUNKS, step, 0)

    part = vg_ref.shape[0]
    for d in range(spaces):
        ws[d, 0] = (vacc[d * part:(d + 1) * part, :] * factor).astype(BF16)
        ws[d, 1] = (oacc[d * part:(d + 1) * part, :] * factor).astype(BF16)
    gacc[...] = gacc[...] * factor

    def w_copy(p):
        d = around(z, p, spaces)
        return remote(ws.at[d], wr.at[z], w_ss.at[p], w_rs.at[z], dev(sec, d))

    def g_copy(p):
        return remote(gacc, gr.at[z], g_ss.at[p], g_rs.at[z], dev(sec, around(z, p, spaces)))

    for p in range(1, spaces):
        g_copy(p).start()
        w_copy(p).start()

    for b in range(spaces):
        src = around(z, b, spaces)

        def pieces(src=src):
            for c in range(CHUNKS):
                remote(iso.at[0], iri.at[src * CHUNKS + c], i_ss.at[0],
                       i_rs.at[src * CHUNKS + c], dev(0, src)).wait_recv()

        if b:
            pieces()
        else:
            pl.when(sec != 0)(pieces)

    def join(y0, carry):
        block = iri[pl.ds(y0 * blocks, blocks)].reshape(size, quarter)
        moved = dot(perm, block, (0, 0)).astype(BF16)
        for r in range(reps):
            ig_ref[pl.ds(pl.multiple_of(r * 512 + y0 * 64, 64), 64), :] = (
                moved[r * 64:r * 64 + 64])
        return carry

    lax.fori_loop(0, 8, join, 0)

    own = pl.ds(pl.multiple_of(z * part, part), part)
    v_sum = vacc[own, :] * factor
    o_sum = oacc[own, :] * factor
    g_sum = gacc[...]
    for p in range(1, spaces):
        src = around(z, p, spaces)
        remote(gacc, gr.at[src], g_ss.at[0], g_rs.at[src], dev(sec, src)).wait_recv()
        remote(ws.at[0], wr.at[src], w_ss.at[0], w_rs.at[src], dev(sec, src)).wait_recv()
        v_sum += wr[src, 0].astype(F32)
        o_sum += wr[src, 1].astype(F32)
        g_sum += gr[src]
    vg_ref[...] = v_sum
    og_ref[...] = o_sum
    gg_ref[...] = g_sum[0:1]

    for p in range(1, spaces):
        g_copy(p).wait_send()
        w_copy(p).wait_send()
        cot_copy(p).wait_send()

    def sent_x(c, carry):
        for p in range(1, spaces):
            x_copy(p, c).wait_send()
        return carry

    lax.fori_loop(0, CHUNKS, sent_x, 0)

    @pl.when(sec != last)
    def _():
        cot_copy(0).wait_send()

    def sent(c, carry):
        @pl.when(sec != 0)
        def _():
            chain_copy(c).wait_send()

        @pl.when(sec == 0)
        def _():
            for a in range(sections):
                for b in range(spaces):
                    if a or b:
                        out_copy(c, a, b).wait_send()
        return carry

    lax.fori_loop(0, CHUNKS, sent, 0)


def fused_call(x, q, k, wv, wo, gain, cot):
    sections = lax.axis_size("section")
    spaces = lax.axis_size("space")
    tok, width = x.shape
    quarter = cot.shape[1]
    reps = tok // COLS // 8
    windows = q.shape[0]
    crow = windows // CHUNKS * reps * 8
    rows = windows // CHUNKS * 64
    part = width // spaces
    factor = float(tok * spaces) ** (-0.5)
    dma = lambda n: pltpu.SemaphoreType.DMA((n,))
    vmem = lambda *shape: pltpu.VMEM(shape, BF16)
    fmem = lambda *shape: pltpu.VMEM(shape, F32)
    sc = spaces * CHUNKS
    full = sections * sc
    return pl.pallas_call(
        functools.partial(fused, sections, spaces, reps, factor),
        out_shape=(
            jax.ShapeDtypeStruct((tok, quarter), BF16),
            jax.ShapeDtypeStruct((part, width), F32),
            jax.ShapeDtypeStruct((part, width), F32),
            jax.ShapeDtypeStruct((1, width), F32),
        ),
        in_specs=[pl.BlockSpec(memory_space=pltpu.VMEM)] * 7,
        out_specs=[pl.BlockSpec(memory_space=pltpu.VMEM)] * 4,
        scratch_shapes=[
            vmem(sc, crow, width), vmem(sc, crow, width),
            vmem(sc, crow, quarter), vmem(sections, spaces, CHUNKS, crow, quarter),
            vmem(CHUNKS, rows, width), vmem(CHUNKS, rows, width),
            vmem(windows * (width // 128), 64, 64 * (128 // HD)),
            fmem(width, width), fmem(width, width), fmem(8, width),
            vmem(full, crow, quarter), vmem(sc, crow, quarter),
            vmem(spaces, 2, part, width), vmem(spaces, 2, part, width),
            fmem(spaces, 8, width),
            dma(sc), dma(sc), dma(spaces), dma(sections * spaces), dma(CHUNKS), dma(CHUNKS),
            dma(full), dma(sc), dma(spaces), dma(spaces), dma(spaces), dma(spaces),
        ],
        compiler_params=pltpu.CompilerParams(
            collective_id=0, has_side_effects=True, vmem_limit_bytes=50 * 2**20),
        cost_estimate=pl.CostEstimate(
            flops=2 * tok * width * width * 5, bytes_accessed=16 * tok * width,
            transcendentals=windows * 64 * 64 * (width // HD)),
    )(x, q, k, wv, wo, gain, cot)


def local(layer_inputs, saved_queries, saved_keys, value_weight, out_weight, norm_gain, cotangent):
    spaces = lax.axis_size("space")
    tok, width = layer_inputs.shape[1:]
    reps = tok // COLS // 8
    fits = (
        reps * 8 * COLS == tok and reps * spaces == 8 and reps >= 2
        and saved_queries.shape[1] % CHUNKS == 0 and cotangent.shape[1] % 128 == 0
        and value_weight.shape[1] == value_weight.shape[2] and width % (128 * spaces) == 0
    )
    if not fits:
        return local_plain(layer_inputs, saved_queries, saved_keys, value_weight, out_weight,
                           norm_gain, cotangent)
    input_grad, value_grad, out_grad, gain_grad = fused_call(
        layer_inputs[0], saved_queries[0], saved_keys[0], value_weight[0], out_weight[0],
        norm_gain, cotangent)
    return (input_grad, value_grad[None], out_grad[None], gain_grad)


def solution(mesh):
    in_specs = (
        P("section", ("groups", "space"), None),
        P("section", ("groups", "space"), None, None),
        P("section", ("groups", "space"), None, None),
        P("section", None, None),
        P("section", None, None),
        P("section", None),
        P(("groups", "space"), "section"),
    )
    out_specs = (
        P(("groups", "space"), "section"),
        P("section", ("groups", "space"), None),
        P("section", ("groups", "space"), None),
        P("section", "groups"),
    )
    return jax.shard_map(local, mesh=mesh, in_specs=in_specs, out_specs=out_specs, check_vma=False)
```

```python
import functools

import jax
import jax.numpy as jnp
from jax import lax
from jax.experimental import pallas as pl
from jax.experimental.pallas import tpu as pltpu
from jax.sharding import PartitionSpec as P

HD = 32
COLS = 64


epsilon = 1e-06


def shifted(block, axis, distance):
    devices = range(lax.axis_size(axis))
    route = [(i - distance, i) for i in devices if i - distance in devices]
    return lax.ppermute(block, axis, route)


def to_pieces(rows_in, band, spaces):
    width = rows_in.shape[-1]
    blocks = rows_in.reshape(band // 8, 8, 8, COLS // 8, width).transpose(1, 3, 0, 2, 4)
    return blocks.reshape(spaces, COLS // spaces, band // 8, 8, width)


def from_pieces(pieces, band, spaces):
    width = pieces.shape[-1]
    depth = band // 8 * spaces // 8
    blocks = pieces.transpose(0, 2, 1, 3, 4).reshape(8, depth, COLS // spaces, 8, width)
    return blocks.transpose(1, 2, 0, 3, 4).reshape(-1, width)


def to_window_pieces(rows_in, band, spaces):
    width = rows_in.shape[-1]
    depth = band // 8 * spaces // 8
    blocks = rows_in.reshape(depth, COLS // spaces, 8, 8, width).transpose(2, 0, 1, 3, 4)
    return blocks.reshape(spaces, band // 8, COLS // spaces, 8, width).transpose(0, 2, 1, 3, 4)


def from_window_pieces(pieces, band):
    width = pieces.shape[-1]
    blocks = pieces.reshape(8, COLS // 8, band // 8, 8, width).transpose(2, 0, 3, 1, 4)
    return blocks.reshape(-1, width)


def window_probs(queries, keys_in):
    count = queries.shape[0]
    heads = queries.shape[-1] // HD
    qv = queries.reshape(count, 64, heads, HD)
    kv = keys_in.reshape(count, 64, heads, HD)
    scores = jnp.einsum("wqhd,wkhd->whqk", qv, kv, preferred_element_type=jnp.float32) * HD ** (
        -0.5
    )
    return jax.nn.softmax(scores, axis=-1).astype(jnp.bfloat16)


def attend(probs, values):
    count = probs.shape[0]
    heads = probs.shape[1]
    grid = values.reshape(count, 64, heads, -1)
    out = jnp.einsum("whqk,wkhd->wqhd", probs, grid, preferred_element_type=jnp.float32)
    return out.reshape(count * 64, -1).astype(jnp.bfloat16)


def attend_back(probs, grads):
    count = probs.shape[0]
    heads = probs.shape[1]
    grid = grads.reshape(count, 64, heads, -1)
    out = jnp.einsum("whqk,wqhd->wkhd", probs, grid, preferred_element_type=jnp.float32)
    return out.reshape(count * 64, -1).astype(jnp.bfloat16)


def inverse_rms(values):
    floats = values.astype(jnp.float32)
    return 1.0 / jnp.sqrt(jnp.mean(floats * floats, axis=-1, keepdims=True) + epsilon)


def local_plain(layer_inputs, saved_queries, saved_keys, value_weight, out_weight, norm_gain, cotangent):
    sections = lax.axis_size("section")
    spaces = lax.axis_size("space")
    section_index = lax.axis_index("section")
    inputs = layer_inputs[0]
    w_value = value_weight[0]
    w_out = out_weight[0]
    gains = norm_gain[0].astype(jnp.float32)
    tok_rows = inputs.shape[0]
    width = inputs.shape[1]
    band = tok_rows // COLS
    factor = float(tok_rows * spaces) ** (-0.5)
    probs = window_probs(saved_queries[0], saved_keys[0])

    def exchange(block):
        return lax.all_to_all(block, "space", split_axis=0, concat_axis=0, tiled=True)

    def to_windows(rows_in):
        return from_pieces(exchange(to_pieces(rows_in, band, spaces)), band, spaces)

    def to_bands(rows_in):
        return from_window_pieces(exchange(to_window_pieces(rows_in, band, spaces)), band)

    cot = lax.all_gather(to_windows(cotangent), "section", axis=1, tiled=True)
    inputs = to_windows(inputs)
    rstd = inverse_rms(inputs)
    normed = inputs.astype(jnp.float32) * rstd
    hidden = (normed * gains).astype(jnp.bfloat16)
    values = jnp.dot(hidden, w_value, preferred_element_type=jnp.float32).astype(jnp.bfloat16)
    attended = attend(probs, values)
    keep_values = jnp.zeros((tok_rows, w_value.shape[1]), jnp.bfloat16)
    keep_cot = jnp.zeros((tok_rows, width), jnp.bfloat16)
    result = cot
    for layer_step in range(sections):
        grad_attn = jnp.dot(cot, w_out, preferred_element_type=jnp.float32).astype(jnp.bfloat16)
        grad_values = attend_back(probs, grad_attn)
        grad_norm = lax.dot_general(
            grad_values, w_value, (((1,), (1,)), ((), ())), preferred_element_type=jnp.float32
        )
        scaled = grad_norm * gains
        total = cot.astype(jnp.float32) + rstd * (
            scaled - normed * jnp.mean(scaled * normed, axis=-1, keepdims=True)
        )
        active = section_index == sections - 1 - layer_step
        keep_values = jnp.where(active, grad_values, keep_values)
        keep_cot = jnp.where(active, cot, keep_cot)
        result = total.astype(jnp.bfloat16)
        if layer_step + 1 < sections:
            cot = shifted(result, "section", -1)
    quarter = width // sections
    split = result.reshape(tok_rows, sections, quarter).transpose(1, 0, 2)
    mine = lax.all_to_all(split, "section", split_axis=0, concat_axis=0, tiled=True)[0]
    input_grad = to_bands(mine)
    kept_norm = lax.dot_general(
        keep_values, w_value, (((1,), (1,)), ((), ())), preferred_element_type=jnp.float32
    )
    gain_part = jnp.sum(kept_norm * normed, axis=0)
    first = lax.dot_general(
        hidden, keep_values, (((0,), (0,)), ((), ())), preferred_element_type=jnp.float32
    )
    second = lax.dot_general(
        keep_cot, attended, (((0,), (0,)), ((), ())), preferred_element_type=jnp.float32
    )
    totals = lax.psum_scatter(
        jnp.concatenate([first, second], axis=1) * factor, "space", scatter_dimension=0, tiled=True
    )
    channels = w_value.shape[1]
    value_grad = totals[:, :channels][None]
    out_grad = totals[:, channels:][None]
    gain_grad = lax.psum(gain_part * factor, "space")[None]
    return (input_grad, value_grad, out_grad, gain_grad)


MESH = pl.DeviceIdType.MESH
CHUNKS = 4
AHEAD = 2
F32 = jnp.float32
BF16 = jnp.bfloat16


def dot(left, right, contract):
    return lax.dot_general(left, right, ((contract[:1], contract[1:]), ((), ())),
                           preferred_element_type=F32)


def fused(sections, spaces, reps, factor,
          x_in, q_in, k_in, wv_in, wo_in, gain_ref, cot_in,
          ig_ref, vg_ref, og_ref, gg_ref,
          cot_ref, x_ref, q_ref, k_ref, wv_ref, wo_ref, l_s,
          xs, xr, cs, cr, ch, res, pt, vacc, oacc, gacc, iso, iri, ws, wr, gr,
          x_ss, x_rs, c_ss, c_rs, h_ss, h_rs, i_ss, i_rs, w_ss, w_rs, g_ss, g_rs):
    sec = lax.axis_index("section")
    z = lax.axis_index("space")
    last = sections - 1
    tile = reps * 8
    windows = q_ref.shape[0]
    wc = windows // CHUNKS
    rows = wc * 64
    crow = wc * tile
    width = x_ref.shape[1]
    quarter = cot_ref.shape[1]
    groups = width // 128

    def dev(s, zz):
        return {"section": s, "space": zz}

    def around(pos, step, size):
        return lax.rem(pos + step, size)

    def remote(src, dst, ssem, rsem, target):
        return pltpu.make_async_remote_copy(
            src_ref=src, dst_ref=dst, send_sem=ssem, recv_sem=rsem,
            device_id=target, device_id_type=MESH)

    def load(i):
        src = (cot_in, x_in, q_in, k_in, wv_in, wo_in)[i]
        dst = (cot_ref, x_ref, q_ref, k_ref, wv_ref, wo_ref)[i]
        return pltpu.make_async_copy(src, dst, l_s.at[i])

    for i in range(6):
        load(i).start()
    barrier = pltpu.get_barrier_semaphore()
    for a in range(sections):
        for b in range(spaces):
            if a or b:
                pl.semaphore_signal(
                    barrier, inc=1,
                    device_id=dev(around(sec, a, sections), around(z, b, spaces)),
                    device_id_type=MESH)

    size = reps * 64
    shift = tile.bit_length() - 1
    row_at = lax.broadcasted_iota(jnp.int32, (size, size), 0)
    col_at = lax.broadcasted_iota(jnp.int32, (size, size), 1)
    wanted = (((row_at >> 3) & (reps - 1)) << 6) + ((row_at & 7) << 3) + (row_at >> shift)
    perm = jnp.where(wanted == col_at, 1.0, 0.0).astype(BF16)
    blocks = size // crow

    def reorder(y0, ref):
        parts = [ref[pl.ds(pl.multiple_of(r * 512 + y0 * 64, 64), 64), :] for r in range(reps)]
        return dot(perm, jnp.concatenate(parts, axis=0), (1, 0)).astype(BF16)

    def split_cot(y0, carry):
        cs[pl.ds(y0 * blocks, blocks)] = reorder(y0, cot_ref).reshape(blocks, crow, quarter)
        return carry

    def split_x(y0, carry):
        xs[pl.ds(y0 * blocks, blocks)] = reorder(y0, x_ref).reshape(blocks, crow, width)
        return carry

    load(0).wait()
    lax.fori_loop(0, 8, split_cot, 0, unroll=4)
    pl.semaphore_wait(barrier, sections * spaces - 1)

    def cot_copy(b):
        d = around(z, b, spaces)
        return remote(cs.at[pl.ds(d * CHUNKS, CHUNKS)], cr.at[sec, z], c_ss.at[b],
                      c_rs.at[sec * spaces + z], dev(last, d))

    for b in range(1, spaces):
        cot_copy(b).start()

    @pl.when(sec != last)
    def _():
        cot_copy(0).start()

    @pl.when(sec == last)
    def _():
        cr[last, z] = cs[pl.ds(z * CHUNKS, CHUNKS)]

    load(1).wait()
    lax.fori_loop(0, 8, split_x, 0, unroll=4)

    def x_copy(p, c):
        d = around(z, p, spaces)
        return remote(xs.at[d * CHUNKS + c], xr.at[z * CHUNKS + c], x_ss.at[p * CHUNKS + c],
                      x_rs.at[z * CHUNKS + c], dev(sec, d))

    def start_x(c, carry):
        for p in range(1, spaces):
            x_copy(p, c).start()
        return carry

    early = lax.rem(sec, 2) == 1

    @pl.when(early)
    def _():
        lax.fori_loop(0, AHEAD, start_x, 0)

    xr[pl.ds(z * CHUNKS, CHUNKS)] = xs[pl.ds(z * CHUNKS, CHUNKS)]

    lane = lax.broadcasted_iota(jnp.int32, (1, 128), 1)
    per = 128 // HD
    heads = [(lane >= h * HD) & (lane < h * HD + HD) for h in range(per)]
    masks = [jnp.where(m, 1.0, 0.0).astype(BF16) for m in heads]

    def spread(block):
        return jnp.concatenate([block * m for m in masks], axis=0)

    def make_probs(w, carry):
        for g in range(groups):
            at = slice(g * 128, g * 128 + 128)
            scores = dot(k_ref[w, :, at], spread(q_ref[w, :, at]), (1, 1)) * HD ** (-0.5)
            top = jnp.max(scores, axis=0, keepdims=True)
            powers = jnp.exp(scores - top)
            pt[w * groups + g] = (
                powers * (1.0 / jnp.sum(powers, axis=0, keepdims=True))).astype(BF16)
        return carry

    load(2).wait()
    load(3).wait()
    lax.fori_loop(0, windows, make_probs, 0, unroll=2)

    @pl.when(jnp.logical_not(early))
    def _():
        lax.fori_loop(0, AHEAD, start_x, 0)

    load(4).wait()
    load(5).wait()
    vacc[...] = jnp.zeros_like(vacc)
    oacc[...] = jnp.zeros_like(oacc)
    gacc[...] = jnp.zeros_like(gacc)

    def out_copy(c, a, b):
        d = around(z, b, spaces)
        return remote(iso.at[(c * sections + a) * spaces + d], iri.at[z * CHUNKS + c],
                      i_ss.at[(c * sections + a) * spaces + b], i_rs.at[z * CHUNKS + c],
                      dev(a, d))

    def chain_copy(c):
        return remote(res.at[c], ch.at[c], h_ss.at[c], h_rs.at[c],
                      dev(lax.rem(sec + last, sections), z))

    @pl.when(sec == last)
    def _():
        for a in range(sections):
            for b in range(spaces):
                src = around(z, b, spaces)

                def arrive(a=a, src=src):
                    remote(cs.at[pl.ds(0, CHUNKS)], cr.at[a, src], c_ss.at[0],
                           c_rs.at[a * spaces + src], dev(a, src)).wait_recv()

                if a != last or b != 0:
                    arrive()
        for c in range(CHUNKS):
            for a in range(sections):
                for u in range(wc):
                    ch[c, u * 64:u * 64 + 64, a * quarter:(a + 1) * quarter] = jnp.concatenate(
                        [cr[a, s, c, u * tile:(u + 1) * tile, :] for s in range(spaces)], axis=0)

    def step(c, carry):
        for p in range(1, spaces):
            src = around(z, p, spaces)
            remote(xs.at[0], xr.at[src * CHUNKS + c], x_ss.at[0], x_rs.at[src * CHUNKS + c],
                   dev(sec, src)).wait_recv()

        @pl.when(c + AHEAD < CHUNKS)
        def _():
            start_x(c + AHEAD, 0)

        parts = [xr[s * CHUNKS + c, u * tile:(u + 1) * tile, :]
                 for u in range(wc) for s in range(spaces)]
        xf = jnp.concatenate(parts, axis=0).astype(F32)
        rstd = 1.0 / jnp.sqrt(jnp.mean(xf * xf, axis=-1, keepdims=True) + epsilon)
        normed = xf * rstd
        gains = gain_ref[...].astype(F32)
        hidden = (normed * gains).astype(BF16)
        values = dot(hidden, wv_ref[...], (1, 0)).astype(BF16)
        out_rows = []
        for w in range(wc):
            out_cols = []
            for g in range(groups):
                full = dot(pt[(c * wc + w) * groups + g],
                           values[w * 64:w * 64 + 64, g * 128:g * 128 + 128], (0, 0))
                one = jnp.where(heads[0], full[:64], 0.0)
                for h in range(1, per):
                    one = jnp.where(heads[h], full[h * 64:h * 64 + 64], one)
                out_cols.append(one.astype(BF16))
            out_rows.append(jnp.concatenate(out_cols, axis=1))
        attended = jnp.concatenate(out_rows, axis=0)

        @pl.when(sec != last)
        def _():
            chain_copy(c).wait_recv()

        cot = ch[c]
        grad_attn = dot(cot, wo_ref[...], (1, 0)).astype(BF16)
        out_rows = []
        for w in range(wc):
            out_cols = []
            for g in range(groups):
                out_cols.append(dot(
                    pt[(c * wc + w) * groups + g],
                    spread(grad_attn[w * 64:w * 64 + 64, g * 128:g * 128 + 128]),
                    (1, 0)).astype(BF16))
            out_rows.append(jnp.concatenate(out_cols, axis=1))
        grad_values = jnp.concatenate(out_rows, axis=0)
        grad_norm = dot(grad_values, wv_ref[...], (1, 1))
        product = grad_norm * normed
        mean = jnp.mean(product * gains, axis=-1, keepdims=True)
        total = cot.astype(F32) + rstd * (grad_norm * gains - normed * mean)
        res[c] = total.astype(BF16)

        @pl.when(sec != 0)
        def _():
            chain_copy(c).start()

        @pl.when(sec == 0)
        def _():
            for a in range(sections):
                for s in range(spaces):
                    iso[(c * sections + a) * spaces + s] = jnp.concatenate(
                        [res[c, u * 64 + s * tile:u * 64 + (s + 1) * tile,
                             a * quarter:(a + 1) * quarter] for u in range(wc)], axis=0)
            for a in range(sections):
                for b in range(spaces):
                    if a or b:
                        out_copy(c, a, b).start()
            iri[z * CHUNKS + c] = iso[c * sections * spaces + z]

        gacc[...] += jnp.sum(product, axis=0, keepdims=True)
        oacc[...] += dot(cot, attended, (0, 0))
        vacc[...] += dot(hidden, grad_values, (0, 0))
        return carry

    lax.fori_loop(0, CHUNKS, step, 0)

    part = vg_ref.shape[0]
    for d in range(spaces):
        ws[d, 0] = (vacc[d * part:(d + 1) * part, :] * factor).astype(BF16)
        ws[d, 1] = (oacc[d * part:(d + 1) * part, :] * factor).astype(BF16)
    gacc[...] = gacc[...] * factor

    def w_copy(p):
        d = around(z, p, spaces)
        return remote(ws.at[d], wr.at[z], w_ss.at[p], w_rs.at[z], dev(sec, d))

    def g_copy(p):
        return remote(gacc, gr.at[z], g_ss.at[p], g_rs.at[z], dev(sec, around(z, p, spaces)))

    for p in range(1, spaces):
        g_copy(p).start()
        w_copy(p).start()

    for b in range(spaces):
        src = around(z, b, spaces)

        def pieces(src=src):
            for c in range(CHUNKS):
                remote(iso.at[0], iri.at[src * CHUNKS + c], i_ss.at[0],
                       i_rs.at[src * CHUNKS + c], dev(0, src)).wait_recv()

        if b:
            pieces()
        else:
            pl.when(sec != 0)(pieces)

    def join(y0, carry):
        block = iri[pl.ds(y0 * blocks, blocks)].reshape(size, quarter)
        moved = dot(perm, block, (0, 0)).astype(BF16)
        for r in range(reps):
            ig_ref[pl.ds(pl.multiple_of(r * 512 + y0 * 64, 64), 64), :] = (
                moved[r * 64:r * 64 + 64])
        return carry

    lax.fori_loop(0, 8, join, 0, unroll=4)

    own = pl.ds(pl.multiple_of(z * part, part), part)
    v_sum = vacc[own, :] * factor
    o_sum = oacc[own, :] * factor
    g_sum = gacc[...]
    for p in range(1, spaces):
        src = around(z, p, spaces)
        remote(gacc, gr.at[src], g_ss.at[0], g_rs.at[src], dev(sec, src)).wait_recv()
        remote(ws.at[0], wr.at[src], w_ss.at[0], w_rs.at[src], dev(sec, src)).wait_recv()
        v_sum += wr[src, 0].astype(F32)
        o_sum += wr[src, 1].astype(F32)
        g_sum += gr[src]
    vg_ref[...] = v_sum
    og_ref[...] = o_sum
    gg_ref[...] = g_sum[0:1]

    for p in range(1, spaces):
        g_copy(p).wait_send()
        w_copy(p).wait_send()
        cot_copy(p).wait_send()

    def sent_x(c, carry):
        for p in range(1, spaces):
            x_copy(p, c).wait_send()
        return carry

    lax.fori_loop(0, CHUNKS, sent_x, 0)

    @pl.when(sec != last)
    def _():
        cot_copy(0).wait_send()

    def sent(c, carry):
        @pl.when(sec != 0)
        def _():
            chain_copy(c).wait_send()

        @pl.when(sec == 0)
        def _():
            for a in range(sections):
                for b in range(spaces):
                    if a or b:
                        out_copy(c, a, b).wait_send()
        return carry

    lax.fori_loop(0, CHUNKS, sent, 0)


def fused_call(x, q, k, wv, wo, gain, cot):
    sections = lax.axis_size("section")
    spaces = lax.axis_size("space")
    tok, width = x.shape
    quarter = cot.shape[1]
    reps = tok // COLS // 8
    windows = q.shape[0]
    crow = windows // CHUNKS * reps * 8
    rows = windows // CHUNKS * 64
    part = width // spaces
    factor = float(tok * spaces) ** (-0.5)
    dma = lambda n: pltpu.SemaphoreType.DMA((n,))
    vmem = lambda *shape: pltpu.VMEM(shape, BF16)
    fmem = lambda *shape: pltpu.VMEM(shape, F32)
    sc = spaces * CHUNKS
    full = sections * sc
    return pl.pallas_call(
        functools.partial(fused, sections, spaces, reps, factor),
        out_shape=(
            jax.ShapeDtypeStruct((tok, quarter), BF16),
            jax.ShapeDtypeStruct((part, width), F32),
            jax.ShapeDtypeStruct((part, width), F32),
            jax.ShapeDtypeStruct((1, width), F32),
        ),
        in_specs=[pl.BlockSpec(memory_space=pltpu.VMEM if i == 5 else pltpu.HBM) for i in range(7)],
        out_specs=[pl.BlockSpec(memory_space=pltpu.VMEM)] * 4,
        scratch_shapes=[
            vmem(*cot.shape), vmem(*x.shape), vmem(*q.shape), vmem(*k.shape), vmem(*wv.shape),
            vmem(*wo.shape), dma(6),
            vmem(sc, crow, width), vmem(sc, crow, width),
            vmem(sc, crow, quarter), vmem(sections, spaces, CHUNKS, crow, quarter),
            vmem(CHUNKS, rows, width), vmem(CHUNKS, rows, width),
            vmem(windows * (width // 128), 64, 64 * (128 // HD)),
            fmem(width, width), fmem(width, width), fmem(8, width),
            vmem(full, crow, quarter), vmem(sc, crow, quarter),
            vmem(spaces, 2, part, width), vmem(spaces, 2, part, width),
            fmem(spaces, 8, width),
            dma(sc), dma(sc), dma(spaces), dma(sections * spaces), dma(CHUNKS), dma(CHUNKS),
            dma(full), dma(sc), dma(spaces), dma(spaces), dma(spaces), dma(spaces),
        ],
        compiler_params=pltpu.CompilerParams(
            collective_id=0, has_side_effects=True, vmem_limit_bytes=50 * 2**20),
        cost_estimate=pl.CostEstimate(
            flops=2 * tok * width * width * 5, bytes_accessed=16 * tok * width,
            transcendentals=windows * 64 * 64 * (width // HD)),
    )(x, q, k, wv, wo, gain, cot)


def local(layer_inputs, saved_queries, saved_keys, value_weight, out_weight, norm_gain, cotangent):
    spaces = lax.axis_size("space")
    tok, width = layer_inputs.shape[1:]
    reps = tok // COLS // 8
    fits = (
        reps * 8 * COLS == tok and reps * spaces == 8 and reps >= 2
        and saved_queries.shape[1] % CHUNKS == 0 and cotangent.shape[1] % 128 == 0
        and value_weight.shape[1] == value_weight.shape[2] and width % (128 * spaces) == 0
    )
    if not fits:
        return local_plain(layer_inputs, saved_queries, saved_keys, value_weight, out_weight,
                           norm_gain, cotangent)
    input_grad, value_grad, out_grad, gain_grad = fused_call(
        layer_inputs[0], saved_queries[0], saved_keys[0], value_weight[0], out_weight[0],
        norm_gain, cotangent)
    return (input_grad, value_grad[None], out_grad[None], gain_grad)


def solution(mesh):
    in_specs = (
        P("section", ("groups", "space"), None),
        P("section", ("groups", "space"), None, None),
        P("section", ("groups", "space"), None, None),
        P("section", None, None),
        P("section", None, None),
        P("section", None),
        P(("groups", "space"), "section"),
    )
    out_specs = (
        P(("groups", "space"), "section"),
        P("section", ("groups", "space"), None),
        P("section", ("groups", "space"), None),
        P("section", "groups"),
    )
    return jax.shard_map(local, mesh=mesh, in_specs=in_specs, out_specs=out_specs, check_vma=False)
```

```python
import functools

import jax
import jax.numpy as jnp
from jax import lax
from jax.experimental import pallas as pl
from jax.experimental.pallas import tpu as pltpu
from jax.sharding import PartitionSpec as P

HD = 32
COLS = 64


epsilon = 1e-06


def shifted(block, axis, distance):
    devices = range(lax.axis_size(axis))
    route = [(i - distance, i) for i in devices if i - distance in devices]
    return lax.ppermute(block, axis, route)


def to_pieces(rows_in, band, spaces):
    width = rows_in.shape[-1]
    blocks = rows_in.reshape(band // 8, 8, 8, COLS // 8, width).transpose(1, 3, 0, 2, 4)
    return blocks.reshape(spaces, COLS // spaces, band // 8, 8, width)


def from_pieces(pieces, band, spaces):
    width = pieces.shape[-1]
    depth = band // 8 * spaces // 8
    blocks = pieces.transpose(0, 2, 1, 3, 4).reshape(8, depth, COLS // spaces, 8, width)
    return blocks.transpose(1, 2, 0, 3, 4).reshape(-1, width)


def to_window_pieces(rows_in, band, spaces):
    width = rows_in.shape[-1]
    depth = band // 8 * spaces // 8
    blocks = rows_in.reshape(depth, COLS // spaces, 8, 8, width).transpose(2, 0, 1, 3, 4)
    return blocks.reshape(spaces, band // 8, COLS // spaces, 8, width).transpose(0, 2, 1, 3, 4)


def from_window_pieces(pieces, band):
    width = pieces.shape[-1]
    blocks = pieces.reshape(8, COLS // 8, band // 8, 8, width).transpose(2, 0, 3, 1, 4)
    return blocks.reshape(-1, width)


def window_probs(queries, keys_in):
    count = queries.shape[0]
    heads = queries.shape[-1] // HD
    qv = queries.reshape(count, 64, heads, HD)
    kv = keys_in.reshape(count, 64, heads, HD)
    scores = jnp.einsum("wqhd,wkhd->whqk", qv, kv, preferred_element_type=jnp.float32) * HD ** (
        -0.5
    )
    return jax.nn.softmax(scores, axis=-1).astype(jnp.bfloat16)


def attend(probs, values):
    count = probs.shape[0]
    heads = probs.shape[1]
    grid = values.reshape(count, 64, heads, -1)
    out = jnp.einsum("whqk,wkhd->wqhd", probs, grid, preferred_element_type=jnp.float32)
    return out.reshape(count * 64, -1).astype(jnp.bfloat16)


def attend_back(probs, grads):
    count = probs.shape[0]
    heads = probs.shape[1]
    grid = grads.reshape(count, 64, heads, -1)
    out = jnp.einsum("whqk,wqhd->wkhd", probs, grid, preferred_element_type=jnp.float32)
    return out.reshape(count * 64, -1).astype(jnp.bfloat16)


def inverse_rms(values):
    floats = values.astype(jnp.float32)
    return 1.0 / jnp.sqrt(jnp.mean(floats * floats, axis=-1, keepdims=True) + epsilon)


def local_plain(layer_inputs, saved_queries, saved_keys, value_weight, out_weight, norm_gain, cotangent):
    sections = lax.axis_size("section")
    spaces = lax.axis_size("space")
    section_index = lax.axis_index("section")
    inputs = layer_inputs[0]
    w_value = value_weight[0]
    w_out = out_weight[0]
    gains = norm_gain[0].astype(jnp.float32)
    tok_rows = inputs.shape[0]
    width = inputs.shape[1]
    band = tok_rows // COLS
    factor = float(tok_rows * spaces) ** (-0.5)
    probs = window_probs(saved_queries[0], saved_keys[0])

    def exchange(block):
        return lax.all_to_all(block, "space", split_axis=0, concat_axis=0, tiled=True)

    def to_windows(rows_in):
        return from_pieces(exchange(to_pieces(rows_in, band, spaces)), band, spaces)

    def to_bands(rows_in):
        return from_window_pieces(exchange(to_window_pieces(rows_in, band, spaces)), band)

    cot = lax.all_gather(to_windows(cotangent), "section", axis=1, tiled=True)
    inputs = to_windows(inputs)
    rstd = inverse_rms(inputs)
    normed = inputs.astype(jnp.float32) * rstd
    hidden = (normed * gains).astype(jnp.bfloat16)
    values = jnp.dot(hidden, w_value, preferred_element_type=jnp.float32).astype(jnp.bfloat16)
    attended = attend(probs, values)
    keep_values = jnp.zeros((tok_rows, w_value.shape[1]), jnp.bfloat16)
    keep_cot = jnp.zeros((tok_rows, width), jnp.bfloat16)
    result = cot
    for layer_step in range(sections):
        grad_attn = jnp.dot(cot, w_out, preferred_element_type=jnp.float32).astype(jnp.bfloat16)
        grad_values = attend_back(probs, grad_attn)
        grad_norm = lax.dot_general(
            grad_values, w_value, (((1,), (1,)), ((), ())), preferred_element_type=jnp.float32
        )
        scaled = grad_norm * gains
        total = cot.astype(jnp.float32) + rstd * (
            scaled - normed * jnp.mean(scaled * normed, axis=-1, keepdims=True)
        )
        active = section_index == sections - 1 - layer_step
        keep_values = jnp.where(active, grad_values, keep_values)
        keep_cot = jnp.where(active, cot, keep_cot)
        result = total.astype(jnp.bfloat16)
        if layer_step + 1 < sections:
            cot = shifted(result, "section", -1)
    quarter = width // sections
    split = result.reshape(tok_rows, sections, quarter).transpose(1, 0, 2)
    mine = lax.all_to_all(split, "section", split_axis=0, concat_axis=0, tiled=True)[0]
    input_grad = to_bands(mine)
    kept_norm = lax.dot_general(
        keep_values, w_value, (((1,), (1,)), ((), ())), preferred_element_type=jnp.float32
    )
    gain_part = jnp.sum(kept_norm * normed, axis=0)
    first = lax.dot_general(
        hidden, keep_values, (((0,), (0,)), ((), ())), preferred_element_type=jnp.float32
    )
    second = lax.dot_general(
        keep_cot, attended, (((0,), (0,)), ((), ())), preferred_element_type=jnp.float32
    )
    totals = lax.psum_scatter(
        jnp.concatenate([first, second], axis=1) * factor, "space", scatter_dimension=0, tiled=True
    )
    channels = w_value.shape[1]
    value_grad = totals[:, :channels][None]
    out_grad = totals[:, channels:][None]
    gain_grad = lax.psum(gain_part * factor, "space")[None]
    return (input_grad, value_grad, out_grad, gain_grad)


MESH = pl.DeviceIdType.MESH
CHUNKS = 4
AHEAD = 2
F32 = jnp.float32
BF16 = jnp.bfloat16


def dot(left, right, contract):
    return lax.dot_general(left, right, ((contract[:1], contract[1:]), ((), ())),
                           preferred_element_type=F32)


def fused(sections, spaces, reps, factor,
          x_in, q_in, k_in, wv_in, wo_in, gain_ref, cot_in,
          ig_ref, vg_ref, og_ref, gg_ref,
          cot_ref, x_ref, q_ref, k_ref, wv_ref, wo_ref, l_s,
          xs, xr, cs, cr, ch, res, pt, vacc, oacc, gacc, iso, iri, ws, wr, gr,
          x_ss, x_rs, c_ss, c_rs, h_ss, h_rs, i_ss, i_rs, w_ss, w_rs, g_ss, g_rs):
    sec = lax.axis_index("section")
    z = lax.axis_index("space")
    last = sections - 1
    tile = reps * 8
    windows = q_ref.shape[0]
    wc = windows // CHUNKS
    rows = wc * 64
    crow = wc * tile
    width = x_ref.shape[1]
    quarter = cot_ref.shape[1]
    groups = width // 128

    def dev(s, zz):
        return {"section": s, "space": zz}

    def around(pos, step, size):
        return lax.rem(pos + step, size)

    def remote(src, dst, ssem, rsem, target):
        return pltpu.make_async_remote_copy(
            src_ref=src, dst_ref=dst, send_sem=ssem, recv_sem=rsem,
            device_id=target, device_id_type=MESH)

    def load(i):
        src = (cot_in, x_in, q_in, k_in, wv_in, wo_in)[i]
        dst = (cot_ref, x_ref, q_ref, k_ref, wv_ref, wo_ref)[i]
        return pltpu.make_async_copy(src, dst, l_s.at[i])

    for i in range(6):
        load(i).start()
    barrier = pltpu.get_barrier_semaphore()
    for a in range(sections):
        for b in range(spaces):
            if a or b:
                pl.semaphore_signal(
                    barrier, inc=1,
                    device_id=dev(around(sec, a, sections), around(z, b, spaces)),
                    device_id_type=MESH)

    size = reps * 64
    shift = tile.bit_length() - 1
    row_at = lax.broadcasted_iota(jnp.int32, (size, size), 0)
    col_at = lax.broadcasted_iota(jnp.int32, (size, size), 1)
    wanted = (((row_at >> 3) & (reps - 1)) << 6) + ((row_at & 7) << 3) + (row_at >> shift)
    perm = jnp.where(wanted == col_at, 1.0, 0.0).astype(BF16)
    blocks = size // crow

    def reorder(y0, ref):
        parts = [ref[pl.ds(pl.multiple_of(r * 512 + y0 * 64, 64), 64), :] for r in range(reps)]
        return dot(perm, jnp.concatenate(parts, axis=0), (1, 0)).astype(BF16)

    def split_cot(y0, carry):
        cs[pl.ds(y0 * blocks, blocks)] = reorder(y0, cot_ref).reshape(blocks, crow, quarter)
        return carry

    def split_x(y0, carry):
        xs[pl.ds(y0 * blocks, blocks)] = reorder(y0, x_ref).reshape(blocks, crow, width)
        return carry

    load(0).wait()
    lax.fori_loop(0, 8, split_cot, 0, unroll=4)
    pl.semaphore_wait(barrier, sections * spaces - 1)

    def cot_copy(b):
        d = around(z, b, spaces)
        return remote(cs.at[pl.ds(d * CHUNKS, CHUNKS)], cr.at[sec, z], c_ss.at[b],
                      c_rs.at[sec * spaces + z], dev(last, d))

    for b in range(1, spaces):
        cot_copy(b).start()

    @pl.when(sec != last)
    def _():
        cot_copy(0).start()

    @pl.when(sec == last)
    def _():
        cr[last, z] = cs[pl.ds(z * CHUNKS, CHUNKS)]

    load(1).wait()
    lax.fori_loop(0, 8, split_x, 0, unroll=4)

    def x_copy(p, c):
        d = around(z, p, spaces)
        return remote(xs.at[d * CHUNKS + c], xr.at[z * CHUNKS + c], x_ss.at[p * CHUNKS + c],
                      x_rs.at[z * CHUNKS + c], dev(sec, d))

    def start_x(c, carry):
        for p in range(1, spaces):
            x_copy(p, c).start()
        return carry

    early = lax.rem(sec, 2) == 1

    @pl.when(early)
    def _():
        lax.fori_loop(0, AHEAD, start_x, 0)

    xr[pl.ds(z * CHUNKS, CHUNKS)] = xs[pl.ds(z * CHUNKS, CHUNKS)]

    lane = lax.broadcasted_iota(jnp.int32, (1, 128), 1)
    per = 128 // HD
    heads = [(lane >= h * HD) & (lane < h * HD + HD) for h in range(per)]
    masks = [jnp.where(m, 1.0, 0.0).astype(BF16) for m in heads]

    def spread(block):
        return jnp.concatenate([block * m for m in masks], axis=0)

    def make_probs(w, carry):
        for g in range(groups):
            at = slice(g * 128, g * 128 + 128)
            scores = dot(k_ref[w, :, at], spread(q_ref[w, :, at]), (1, 1)) * HD ** (-0.5)
            top = jnp.max(scores, axis=0, keepdims=True)
            powers = jnp.exp(scores - top)
            pt[w * groups + g] = (
                powers * (1.0 / jnp.sum(powers, axis=0, keepdims=True))).astype(BF16)
        return carry

    load(2).wait()
    load(3).wait()
    lax.fori_loop(0, windows, make_probs, 0, unroll=2)

    @pl.when(jnp.logical_not(early))
    def _():
        lax.fori_loop(0, AHEAD, start_x, 0)

    load(4).wait()
    load(5).wait()
    vacc[...] = jnp.zeros_like(vacc)
    oacc[...] = jnp.zeros_like(oacc)
    gacc[...] = jnp.zeros_like(gacc)

    def out_copy(c, a, b):
        d = around(z, b, spaces)
        return remote(iso.at[(c * sections + a) * spaces + d], iri.at[z * CHUNKS + c],
                      i_ss.at[(c * sections + a) * spaces + b], i_rs.at[z * CHUNKS + c],
                      dev(a, d))

    def chain_copy(c):
        return remote(res.at[c], ch.at[c], h_ss.at[c], h_rs.at[c],
                      dev(lax.rem(sec + last, sections), z))

    @pl.when(sec == last)
    def _():
        for a in range(sections):
            for b in range(spaces):
                src = around(z, b, spaces)

                def arrive(a=a, src=src):
                    remote(cs.at[pl.ds(0, CHUNKS)], cr.at[a, src], c_ss.at[0],
                           c_rs.at[a * spaces + src], dev(a, src)).wait_recv()

                if a != last or b != 0:
                    arrive()
        for c in range(CHUNKS):
            for a in range(sections):
                for u in range(wc):
                    ch[c, u * 64:u * 64 + 64, a * quarter:(a + 1) * quarter] = jnp.concatenate(
                        [cr[a, s, c, u * tile:(u + 1) * tile, :] for s in range(spaces)], axis=0)

    def step(c, carry):
        for p in range(1, spaces):
            src = around(z, p, spaces)
            remote(xs.at[0], xr.at[src * CHUNKS + c], x_ss.at[0], x_rs.at[src * CHUNKS + c],
                   dev(sec, src)).wait_recv()

        @pl.when(c + AHEAD < CHUNKS)
        def _():
            start_x(c + AHEAD, 0)

        parts = [xr[s * CHUNKS + c, u * tile:(u + 1) * tile, :]
                 for u in range(wc) for s in range(spaces)]
        xf = jnp.concatenate(parts, axis=0).astype(F32)
        rstd = 1.0 / jnp.sqrt(jnp.mean(xf * xf, axis=-1, keepdims=True) + epsilon)
        normed = xf * rstd
        gains = gain_ref[...].astype(F32)
        hidden = (normed * gains).astype(BF16)
        values = dot(hidden, wv_ref[...], (1, 0)).astype(BF16)
        out_rows = []
        for w in range(wc):
            out_cols = []
            for g in range(groups):
                full = dot(pt[(c * wc + w) * groups + g],
                           values[w * 64:w * 64 + 64, g * 128:g * 128 + 128], (0, 0))
                one = jnp.where(heads[0], full[:64], 0.0)
                for h in range(1, per):
                    one = jnp.where(heads[h], full[h * 64:h * 64 + 64], one)
                out_cols.append(one.astype(BF16))
            out_rows.append(jnp.concatenate(out_cols, axis=1))
        attended = jnp.concatenate(out_rows, axis=0)

        @pl.when(sec != last)
        def _():
            chain_copy(c).wait_recv()

        cot = ch[c]
        grad_attn = dot(cot, wo_ref[...], (1, 0)).astype(BF16)
        out_rows = []
        for w in range(wc):
            out_cols = []
            for g in range(groups):
                out_cols.append(dot(
                    pt[(c * wc + w) * groups + g],
                    spread(grad_attn[w * 64:w * 64 + 64, g * 128:g * 128 + 128]),
                    (1, 0)).astype(BF16))
            out_rows.append(jnp.concatenate(out_cols, axis=1))
        grad_values = jnp.concatenate(out_rows, axis=0)
        grad_norm = dot(grad_values, wv_ref[...], (1, 1))
        product = grad_norm * normed
        mean = jnp.mean(product * gains, axis=-1, keepdims=True)
        total = cot.astype(F32) + rstd * (grad_norm * gains - normed * mean)
        res[c] = total.astype(BF16)

        @pl.when(sec != 0)
        def _():
            chain_copy(c).start()

        @pl.when(sec == 0)
        def _():
            for a in range(sections):
                for s in range(spaces):
                    iso[(c * sections + a) * spaces + s] = jnp.concatenate(
                        [res[c, u * 64 + s * tile:u * 64 + (s + 1) * tile,
                             a * quarter:(a + 1) * quarter] for u in range(wc)], axis=0)
            for a in range(sections):
                for b in range(spaces):
                    if a or b:
                        out_copy(c, a, b).start()
            iri[z * CHUNKS + c] = iso[c * sections * spaces + z]

        gacc[...] += jnp.sum(product, axis=0, keepdims=True)
        oacc[...] += dot(cot, attended, (0, 0))
        vacc[...] += dot(hidden, grad_values, (0, 0))
        return carry

    lax.fori_loop(0, CHUNKS, step, 0)

    part = vg_ref.shape[0]
    gacc[...] = gacc[...] * factor

    def w_copy(p):
        d = around(z, p, spaces)
        return remote(ws.at[d], wr.at[z], w_ss.at[p], w_rs.at[z], dev(sec, d))

    def g_copy(p):
        return remote(gacc, gr.at[z], g_ss.at[p], g_rs.at[z], dev(sec, around(z, p, spaces)))

    for p in range(1, spaces):
        d = around(z, p, spaces)
        rows_of = pl.ds(pl.multiple_of(d * part, part), part)
        ws[d, 0] = (vacc[rows_of, :] * factor).astype(BF16)
        ws[d, 1] = (oacc[rows_of, :] * factor).astype(BF16)
        w_copy(p).start()
    for p in range(1, spaces):
        g_copy(p).start()

    for b in range(spaces):
        src = around(z, b, spaces)

        def pieces(src=src):
            for c in range(CHUNKS):
                remote(iso.at[0], iri.at[src * CHUNKS + c], i_ss.at[0],
                       i_rs.at[src * CHUNKS + c], dev(0, src)).wait_recv()

        if b:
            pieces()
        else:
            pl.when(sec != 0)(pieces)

    def join(y0, carry):
        block = iri[pl.ds(y0 * blocks, blocks)].reshape(size, quarter)
        moved = dot(perm, block, (0, 0)).astype(BF16)
        for r in range(reps):
            ig_ref[pl.ds(pl.multiple_of(r * 512 + y0 * 64, 64), 64), :] = (
                moved[r * 64:r * 64 + 64])
        return carry

    lax.fori_loop(0, 8, join, 0, unroll=4)

    own = pl.ds(pl.multiple_of(z * part, part), part)
    v_sum = vacc[own, :] * factor
    o_sum = oacc[own, :] * factor
    g_sum = gacc[...]
    for p in range(1, spaces):
        src = around(z, p, spaces)
        remote(gacc, gr.at[src], g_ss.at[0], g_rs.at[src], dev(sec, src)).wait_recv()
        remote(ws.at[0], wr.at[src], w_ss.at[0], w_rs.at[src], dev(sec, src)).wait_recv()
        v_sum += wr[src, 0].astype(F32)
        o_sum += wr[src, 1].astype(F32)
        g_sum += gr[src]
    vg_ref[...] = v_sum
    og_ref[...] = o_sum
    gg_ref[...] = g_sum[0:1]

    for p in range(1, spaces):
        g_copy(p).wait_send()
        w_copy(p).wait_send()
        cot_copy(p).wait_send()

    def sent_x(c, carry):
        for p in range(1, spaces):
            x_copy(p, c).wait_send()
        return carry

    lax.fori_loop(0, CHUNKS, sent_x, 0)

    @pl.when(sec != last)
    def _():
        cot_copy(0).wait_send()

    def sent(c, carry):
        @pl.when(sec != 0)
        def _():
            chain_copy(c).wait_send()

        @pl.when(sec == 0)
        def _():
            for a in range(sections):
                for b in range(spaces):
                    if a or b:
                        out_copy(c, a, b).wait_send()
        return carry

    lax.fori_loop(0, CHUNKS, sent, 0)


def fused_call(x, q, k, wv, wo, gain, cot):
    sections = lax.axis_size("section")
    spaces = lax.axis_size("space")
    tok, width = x.shape
    quarter = cot.shape[1]
    reps = tok // COLS // 8
    windows = q.shape[0]
    crow = windows // CHUNKS * reps * 8
    rows = windows // CHUNKS * 64
    part = width // spaces
    factor = float(tok * spaces) ** (-0.5)
    dma = lambda n: pltpu.SemaphoreType.DMA((n,))
    vmem = lambda *shape: pltpu.VMEM(shape, BF16)
    fmem = lambda *shape: pltpu.VMEM(shape, F32)
    sc = spaces * CHUNKS
    full = sections * sc
    return pl.pallas_call(
        functools.partial(fused, sections, spaces, reps, factor),
        out_shape=(
            jax.ShapeDtypeStruct((tok, quarter), BF16),
            jax.ShapeDtypeStruct((part, width), F32),
            jax.ShapeDtypeStruct((part, width), F32),
            jax.ShapeDtypeStruct((1, width), F32),
        ),
        in_specs=[pl.BlockSpec(memory_space=pltpu.VMEM if i == 5 else pltpu.HBM) for i in range(7)],
        out_specs=[pl.BlockSpec(memory_space=pltpu.VMEM)] * 4,
        scratch_shapes=[
            vmem(*cot.shape), vmem(*x.shape), vmem(*q.shape), vmem(*k.shape), vmem(*wv.shape),
            vmem(*wo.shape), dma(6),
            vmem(sc, crow, width), vmem(sc, crow, width),
            vmem(sc, crow, quarter), vmem(sections, spaces, CHUNKS, crow, quarter),
            vmem(CHUNKS, rows, width), vmem(CHUNKS, rows, width),
            vmem(windows * (width // 128), 64, 64 * (128 // HD)),
            fmem(width, width), fmem(width, width), fmem(8, width),
            vmem(full, crow, quarter), vmem(sc, crow, quarter),
            vmem(spaces, 2, part, width), vmem(spaces, 2, part, width),
            fmem(spaces, 8, width),
            dma(sc), dma(sc), dma(spaces), dma(sections * spaces), dma(CHUNKS), dma(CHUNKS),
            dma(full), dma(sc), dma(spaces), dma(spaces), dma(spaces), dma(spaces),
        ],
        compiler_params=pltpu.CompilerParams(
            collective_id=0, has_side_effects=True, vmem_limit_bytes=50 * 2**20),
        cost_estimate=pl.CostEstimate(
            flops=2 * tok * width * width * 5, bytes_accessed=16 * tok * width,
            transcendentals=windows * 64 * 64 * (width // HD)),
    )(x, q, k, wv, wo, gain, cot)


def local(layer_inputs, saved_queries, saved_keys, value_weight, out_weight, norm_gain, cotangent):
    spaces = lax.axis_size("space")
    tok, width = layer_inputs.shape[1:]
    reps = tok // COLS // 8
    fits = (
        reps * 8 * COLS == tok and reps * spaces == 8 and reps >= 2
        and saved_queries.shape[1] % CHUNKS == 0 and cotangent.shape[1] % 128 == 0
        and value_weight.shape[1] == value_weight.shape[2] and width % (128 * spaces) == 0
    )
    if not fits:
        return local_plain(layer_inputs, saved_queries, saved_keys, value_weight, out_weight,
                           norm_gain, cotangent)
    input_grad, value_grad, out_grad, gain_grad = fused_call(
        layer_inputs[0], saved_queries[0], saved_keys[0], value_weight[0], out_weight[0],
        norm_gain, cotangent)
    return (input_grad, value_grad[None], out_grad[None], gain_grad)


def solution(mesh):
    in_specs = (
        P("section", ("groups", "space"), None),
        P("section", ("groups", "space"), None, None),
        P("section", ("groups", "space"), None, None),
        P("section", None, None),
        P("section", None, None),
        P("section", None),
        P(("groups", "space"), "section"),
    )
    out_specs = (
        P(("groups", "space"), "section"),
        P("section", ("groups", "space"), None),
        P("section", ("groups", "space"), None),
        P("section", "groups"),
    )
    return jax.shard_map(local, mesh=mesh, in_specs=in_specs, out_specs=out_specs, check_vma=False)
```
